32 devices in a mesh: lsec: 4 (over y, core), rsec: 8 (over z, x).
Axes of the slice: x: 2, y: 2, z: 4, core: 2. Of those that a mesh axis runs over, the one named last changes fastest.
Arguments:
- two_site: bfloat16 [2, 16, 128, 4096], P(None, 'lsec', None, 'rsec'), may hold values from -6 to 6
- left_env: bfloat16 [34, 16, 128, 128], P(None, 'lsec', 'rsec'), may hold values from -0.09375 to 0.09375
- right_env: bfloat16 [34, 32, 128, 128], P(None, 'rsec', 'lsec'), may hold values from -0.5 to 0.5
- left_size: int32 [16], P('lsec'), may hold values from 16 to 128, as said below
- right_size: int32 [32], P('rsec'), may hold values from 16 to 128, as said below
- channel_shift: int32 [34, 2], replicated, may hold values from -2 to 2, as said below
Outputs:
- applied: bfloat16 [2, 16, 128, 4096], P(None, 'lsec', None, 'rsec')
The draws below stay inside these ranges and needn't reach their ends.
Inputs may be any that keep to these rules, and one draw needn't show every extreme that they name: `left_size`: each sector holds 16 to 128 states; some left sector and some right sector hold exactly 128. `right_size`: as for left_size. `channel_shift`: every offset from -2 to 2 is the left offset of some channel and the right offset of some channel.
All inputs are finite; a program needn't handle non-finite values.
Results may differ from the reference program's by a relative error of at most 0.0049.
Values may be sent and summed in bfloat16 or wider, within the bound.
A program may use at most 64 MiB of HBM per device.

```python
import jax
import jax.numpy as jnp
from jax import lax

SB = 128
KCH = 34
VECS = 2
SHIFT = 2
NL = 16
NR = 32
DL = 2048
DR = 4096


def sector_sizes(key, count):
    sizes = jax.random.randint(key, (count,), SB // 8, SB + 1)
    spot = jax.random.randint(jax.random.fold_in(key, 7), (), 0, count)
    return sizes.at[spot].set(SB).astype(jnp.int32)


def draw_left_size(key, part):
    return sector_sizes(jax.random.fold_in(key, 11), NL)


def draw_right_size(key, part):
    return sector_sizes(jax.random.fold_in(key, 13), NR)


def draw_channel_shift(key, part):
    spread = 2 * SHIFT + 1
    left_part = jax.random.permutation(jax.random.fold_in(key, 1), KCH) % spread - SHIFT
    right_part = jax.random.permutation(jax.random.fold_in(key, 2), KCH) % spread - SHIFT
    return jnp.stack([left_part, right_part], axis=1).astype(jnp.int32)


def block_levels(key, extent, split, smallest, largest):
    factor_of, own = 1.0, jax.random.fold_in(key, 6)
    for axis_at, shards_of in split:
        draws = jnp.exp(jax.random.uniform(jax.random.fold_in(own, axis_at), (shards_of,), jnp.float32, smallest / len(split), largest / len(split)))
        factor_of = factor_of * jnp.repeat(draws, extent[axis_at] // shards_of).reshape([-1 if axis == axis_at else 1 for axis in range(len(extent))])
    return factor_of


def bell_draw(rng, extent, scale, bound, pieces=(), held_as=jnp.bfloat16):
    drawn = scale * jax.random.normal(rng, extent, jnp.float32)
    if pieces:
        drawn = drawn * block_levels(rng, extent, pieces, -0.22, 0.18)
    return jnp.clip(drawn, -bound, bound).astype(held_as)


def setup_inputs(seed: int = 0) -> dict:
    streams_of = jax.random.split(jax.random.key(seed), 7)
    two_site = bell_draw(streams_of[0], (VECS, NL, SB, DR), 1.0, 6.0, ((1, 4), (3, 8)))
    left_env = bell_draw(streams_of[1], (KCH, NL, SB, SB), (SB * KCH) ** -0.5, 0.09375, ((1, 4), (2, 8)))
    right_env = bell_draw(streams_of[2], (KCH, NR, SB, SB), SB ** -0.5, 0.5, ((1, 8), (2, 4)))
    left_size = draw_left_size(jax.random.fold_in(streams_of[6], 71), 0)
    right_size = draw_right_size(jax.random.fold_in(streams_of[6], 71), 0)
    channel_shift = draw_channel_shift(jax.random.fold_in(streams_of[6], 71), 0)
    return {"two_site": two_site, "left_env": left_env, "right_env": right_env, "left_size": left_size, "right_size": right_size, "channel_shift": channel_shift}


def live_states(sizes, count):
    states = jnp.arange(SB, dtype=jnp.int32)
    return (states[None, :] < sizes[:, None]).astype(jnp.float32).reshape(count * SB)


def reference(two_site, left_env, right_env, left_size, right_size, channel_shift):
    row_live = live_states(left_size, NL)
    col_live = live_states(right_size, NR)
    weights = row_live[:, None] * col_live[None, :]
    masked = (two_site.astype(jnp.float32).reshape(VECS, DL, DR) * weights[None]).reshape(VECS, NL, SB, NR, SB)
    padded = jnp.pad(masked, ((0, 0), (SHIFT, SHIFT), (0, 0), (SHIFT, SHIFT), (0, 0)))
    left_expanded = left_env.astype(jnp.float32)
    right_wide = right_env.astype(jnp.float32)

    def one_channel(operator_bond_index, cumulative_sum):
        left_sector_offset = (SHIFT - channel_shift[operator_bond_index, 0]).astype(jnp.int32)
        right_start = (SHIFT - channel_shift[operator_bond_index, 1]).astype(jnp.int32)
        zero_index = jnp.int32(0)
        source = lax.dynamic_slice(padded, (zero_index, left_sector_offset, zero_index, right_start, zero_index), (VECS, NL, SB, NR, SB))
        right_reduced = jnp.einsum("vlarb,rcb->vlarc", source, right_wide[operator_bond_index]).astype(jnp.bfloat16)
        right_reduced = lax.optimization_barrier(right_reduced).astype(jnp.float32)
        return cumulative_sum + jnp.einsum("jit,xjtum->xjium", left_expanded[operator_bond_index], right_reduced)

    cumulative_sum = lax.fori_loop(0, KCH, one_channel, jnp.zeros((VECS, NL, SB, NR, SB), jnp.float32))
    result = cumulative_sum.reshape(VECS, DL, DR) * weights[None]
    return result.astype(jnp.bfloat16).reshape(VECS, NL, SB, DR)
```

```python
import functools

import jax
import jax.numpy as jnp
from jax import lax
from jax.experimental import pallas as pl
from jax.experimental.pallas import tpu as pltpu
from jax.sharding import PartitionSpec as P

SHIFT = 2
GROUP = 2
AHEAD = 3
MESH = pl.DeviceIdType.MESH


def kernel(
    nl, nr, lsize, rsize, shift, x_hbm, l_hbm, r_hbm, out,
    xbuf, lbuf, rbuf, pbuf, acc,
    x_sem, own_sem, rh_send, rh_recv, lh_send, lh_recv,
    l1_send, l1_recv, l2_send, l2_recv, r1_send, r1_recv, r2_send, r2_recv,
):
    vectors, lc, sb, columns = x_hbm.shape
    rc = columns // sb
    channels = l_hbm.shape[0]
    eb = l_hbm.shape[1] // lc
    cb = r_hbm.shape[1] // rc
    chunks = channels // GROUP
    nz, ny = nr // 2, nl // 2
    lam = lax.axis_index("lsec")
    rho = lax.axis_index("rsec")
    mz, mx = rho // 2, rho % 2
    my, mc = lam // 2, lam % 2
    xpeer = mz * 2 + (1 - mx)
    cpeer = my * 2 + (1 - mc)
    S = SHIFT
    own_r, own_l = pl.ds(S, rc), pl.ds(S, lc)

    def zslot(j):
        return ((mz + (nz - j)) % nz) * 2 + mx

    def yslot(j):
        return ((my + (ny - j)) % ny) * 2 + mc

    def zto(j):
        return ((mz + j) % nz) * 2 + mx

    def yto(j):
        return ((my + j) % ny) * 2 + mc

    def remote(src, dst, send, recv, to):
        return pltpu.make_async_remote_copy(
            src_ref=src, dst_ref=dst, send_sem=send, recv_sem=recv,
            device_id=to, device_id_type=MESH,
        )

    x_copies = [
        pltpu.make_async_copy(
            x_hbm.at[:, :, :, pl.ds(r * sb, sb)], xbuf.at[S + r, :, own_l], x_sem.at[r]
        )
        for r in range(rc)
    ]
    for copy in x_copies:
        copy.start()
    own_l_copy = pltpu.make_async_copy(l_hbm, lbuf.at[rho], own_sem.at[0])
    own_r_copy = pltpu.make_async_copy(r_hbm, rbuf.at[lam], own_sem.at[1])
    own_l_copy.start()
    own_r_copy.start()

    has_up_r, has_dn_r = rho < nr - 1, rho > 0
    has_up_l, has_dn_l = lam < nl - 1, lam > 0
    far_r = jnp.where(mx == 1, rho + 1, rho + nr - 1) % nr
    far_l = jnp.where(mc == 1, lam + 1, lam + nl - 1) % nl

    barrier = pltpu.get_barrier_semaphore()
    near = [(lam, zto(j)) for j in range(1, nz)] + [(lam, xpeer)]
    near += [(yto(j), rho) for j in range(1, ny)] + [(cpeer, rho)]
    near += [(lam, far_r), (far_l, rho)]
    for to in near:
        pl.semaphore_signal(barrier, inc=1, device_id=to, device_id_type=MESH)

    def zero_r(at):
        xbuf[pl.ds(at, S)] = jnp.zeros((S,) + xbuf.shape[1:], xbuf.dtype)

    def zero_l(at):
        shape = (rc + 2 * S, vectors, S, sb, sb)
        xbuf[:, :, pl.ds(at, S)] = jnp.zeros(shape, xbuf.dtype)

    pl.when(rho == 0)(lambda: zero_r(0))
    pl.when(rho == nr - 1)(lambda: zero_r(S + rc))
    pl.when(lam == 0)(lambda: zero_l(0))
    pl.when(lam == nl - 1)(lambda: zero_l(S + lc))

    rows = lax.broadcasted_iota(jnp.int32, (sb, sb), 0)
    cols = lax.broadcasted_iota(jnp.int32, (sb, sb), 1)
    for r in range(rc):
        x_copies[r].wait()
        for l in range(lc):
            live = ((rows < lsize[l]) & (cols < rsize[r])).astype(jnp.float32)
            for v in range(vectors):
                block = xbuf[S + r, v, S + l].astype(jnp.float32)
                xbuf[S + r, v, S + l] = (block * live).astype(xbuf.dtype)

    pl.semaphore_wait(barrier, len(near))

    r_up = remote(
        xbuf.at[pl.ds(rc, S), :, own_l], xbuf.at[pl.ds(0, S), :, own_l],
        rh_send.at[0], rh_recv.at[0], (lam, rho + 1),
    )
    r_dn = remote(
        xbuf.at[pl.ds(S, S), :, own_l], xbuf.at[pl.ds(S + rc, S), :, own_l],
        rh_send.at[1], rh_recv.at[1], (lam, rho - 1),
    )

    def l_rim(part, at, count):
        up = remote(
            xbuf.at[pl.ds(at, count), :, pl.ds(lc, S)], xbuf.at[pl.ds(at, count), :, pl.ds(0, S)],
            lh_send.at[part, 0], lh_recv.at[part, 0], (lam + 1, rho),
        )
        dn = remote(
            xbuf.at[pl.ds(at, count), :, pl.ds(S, S)], xbuf.at[pl.ds(at, count), :, pl.ds(S + lc, S)],
            lh_send.at[part, 1], lh_recv.at[part, 1], (lam - 1, rho),
        )
        return up, dn

    l_mid = l_rim(0, S, rc)
    l_low = l_rim(1, 0, S)
    l_high = l_rim(2, S + rc, S)
    pl.when(has_up_r)(r_up.start)
    pl.when(has_dn_r)(r_dn.start)
    pl.when(has_up_l)(l_mid[0].start)
    pl.when(has_dn_l)(l_mid[1].start)

    def first_hop(c):
        part = pl.ds(c * GROUP, GROUP)
        copies = []
        for j in range(1, nz):
            copies.append(remote(
                l_hbm.at[part], lbuf.at[rho, part],
                l1_send.at[c, j - 1], l1_recv.at[c, j - 1], (lam, zto(j)),
            ))
        for j in range(1, ny):
            copies.append(remote(
                r_hbm.at[part], rbuf.at[lam, part],
                r1_send.at[c, j - 1], r1_recv.at[c, j - 1], (yto(j), rho),
            ))
        copies.append(remote(
            l_hbm.at[part], lbuf.at[rho, part],
            l2_send.at[c, 0], l2_recv.at[c, 0], (lam, xpeer),
        ))
        copies.append(remote(
            r_hbm.at[part], rbuf.at[lam, part],
            r2_send.at[c, 0], r2_recv.at[c, 0], (cpeer, rho),
        ))
        return copies

    def first_in(c):
        part = pl.ds(c * GROUP, GROUP)
        copies = []
        for j in range(1, nz):
            copies.append(remote(
                l_hbm.at[part], lbuf.at[zslot(j), part],
                l1_send.at[c, j - 1], l1_recv.at[c, j - 1], (lam, zto(j)),
            ))
        for j in range(1, ny):
            copies.append(remote(
                r_hbm.at[part], rbuf.at[yslot(j), part],
                r1_send.at[c, j - 1], r1_recv.at[c, j - 1], (yto(j), rho),
            ))
        return copies

    def second_hop(c):
        part = pl.ds(c * GROUP, GROUP)
        copies = []
        for j in range(1, nz):
            at = lbuf.at[zslot(j), part]
            copies.append(remote(at, at, l2_send.at[c, j], l2_recv.at[c, j], (lam, xpeer)))
        for j in range(1, ny):
            at = rbuf.at[yslot(j), part]
            copies.append(remote(at, at, r2_send.at[c, j], r2_recv.at[c, j], (cpeer, rho)))
        return copies

    def second_in(c):
        part = pl.ds(c * GROUP, GROUP)
        copies = []
        for j in range(nz):
            at = lbuf.at[((mz + (nz - j)) % nz) * 2 + (1 - mx), part]
            copies.append(remote(at, at, l2_send.at[c, j], l2_recv.at[c, j], (lam, xpeer)))
        for j in range(ny):
            at = rbuf.at[((my + (ny - j)) % ny) * 2 + (1 - mc), part]
            copies.append(remote(at, at, r2_send.at[c, j], r2_recv.at[c, j], (cpeer, rho)))
        return copies

    def start_first(c):
        for copy in first_hop(c):
            copy.start()

    def forward(c):
        for copy in first_in(c):
            copy.wait_recv()
        for copy in second_hop(c):
            copy.start()

    for c in range(AHEAD):
        start_first(c)

    @pl.when(has_dn_r)
    def _():
        r_up.wait_recv()
        pl.when(has_up_l)(l_low[0].start)
        pl.when(has_dn_l)(l_low[1].start)

    @pl.when(has_up_r)
    def _():
        r_dn.wait_recv()
        pl.when(has_up_l)(l_high[0].start)
        pl.when(has_dn_l)(l_high[1].start)

    acc[...] = jnp.zeros_like(acc)
    own_l_copy.wait()
    own_r_copy.wait()
    forward(0)

    @pl.when(has_dn_l)
    def _():
        l_mid[0].wait_recv()
        pl.when(has_dn_r)(l_low[0].wait_recv)
        pl.when(has_up_r)(l_high[0].wait_recv)

    @pl.when(has_up_l)
    def _():
        l_mid[1].wait_recv()
        pl.when(has_dn_r)(l_low[1].wait_recv)
        pl.when(has_up_r)(l_high[1].wait_recv)

    def right_block(k, r):
        return rbuf[:, k, pl.ds(r * cb, cb), :].reshape(sb, sb)

    def left_block(k, l):
        if eb % 16 == 0:
            return lbuf[:, k, pl.ds(l * eb, eb), :].reshape(sb, sb)
        pieces = lbuf[:, k].astype(jnp.float32).reshape(nr, lc, eb, sb)
        return pieces[:, l].reshape(sb, sb).astype(jnp.bfloat16)

    def step(c, carry):
        @pl.when(c + AHEAD < chunks)
        def _():
            start_first(c + AHEAD)

        @pl.when(c + 1 < chunks)
        def _():
            forward(c + 1)

        for copy in second_in(c):
            copy.wait_recv()
        for g in range(GROUP):
            k = c * GROUP + g
            l_from = S - shift[k, 0]
            r_from = S - shift[k, 1]
            for r in range(rc):
                weights = right_block(k, r)
                for v in range(vectors):
                    source = xbuf[r_from + r, v, pl.ds(l_from, lc)].reshape(lc * sb, sb)
                    part = lax.dot_general(
                        source, weights, (((1,), (1,)), ((), ())),
                        preferred_element_type=jnp.float32,
                    ).astype(jnp.bfloat16)
                    pbuf[:, pl.ds(g * sb, sb), pl.ds((v * rc + r) * sb, sb)] = part.reshape(lc, sb, sb)
        for l in range(lc):
            left = jnp.concatenate(
                [left_block(c * GROUP + g, l) for g in range(GROUP)], axis=1
            )
            acc[l] += jnp.dot(left, pbuf[l], preferred_element_type=jnp.float32)
        return carry

    lax.fori_loop(0, chunks, step, 0)

    for l in range(lc):
        for r in range(rc):
            live = ((rows < lsize[l]) & (cols < rsize[r])).astype(jnp.float32)
            for v in range(vectors):
                block = acc[l, :, pl.ds((v * rc + r) * sb, sb)]
                out[v, l, :, pl.ds(r * sb, sb)] = (block * live).astype(out.dtype)

    def drain(c, carry):
        for copy in first_hop(c) + second_hop(c):
            copy.wait_send()
        return carry

    lax.fori_loop(0, chunks, drain, 0)
    pl.when(has_up_r)(r_up.wait_send)
    pl.when(has_dn_r)(r_dn.wait_send)
    for pair, there in ((l_mid, None), (l_low, has_dn_r), (l_high, has_up_r)):
        for copy, to in zip(pair, (has_up_l, has_dn_l)):
            pl.when(to if there is None else to & there)(copy.wait_send)


def local(nl, nr, two_site, left_env, right_env, left_size, right_size, channel_shift):
    vectors, lc, sb, columns = two_site.shape
    channels, rc = right_env.shape[:2]
    chunks = channels // GROUP
    nz, ny = nr // 2, nl // 2
    left_rows = left_env.reshape(channels, -1, sb)
    right_rows = right_env.reshape(channels, -1, sb)
    smem = pl.BlockSpec(memory_space=pltpu.SMEM)
    hbm = pl.BlockSpec(memory_space=pl.ANY)
    dma = pltpu.SemaphoreType.DMA
    return pl.pallas_call(
        functools.partial(kernel, nl, nr),
        out_shape=jax.ShapeDtypeStruct(two_site.shape, jnp.bfloat16),
        in_specs=[smem, smem, smem, hbm, hbm, hbm],
        out_specs=pl.BlockSpec(memory_space=pltpu.VMEM),
        scratch_shapes=[
            pltpu.VMEM((rc + 2 * SHIFT, vectors, lc + 2 * SHIFT, sb, sb), jnp.bfloat16),
            pltpu.VMEM((nr,) + left_rows.shape, jnp.bfloat16),
            pltpu.VMEM((nl,) + right_rows.shape, jnp.bfloat16),
            pltpu.VMEM((lc, GROUP * sb, vectors * columns), jnp.bfloat16),
            pltpu.VMEM((lc, sb, vectors * columns), jnp.float32),
            dma((rc,)), dma((2,)), dma((2,)), dma((2,)), dma((3, 2)), dma((3, 2)),
            dma((chunks, nz - 1)), dma((chunks, nz - 1)), dma((chunks, nz)), dma((chunks, nz)),
            dma((chunks, ny - 1)), dma((chunks, ny - 1)), dma((chunks, ny)), dma((chunks, ny)),
        ],
        compiler_params=pltpu.CompilerParams(
            collective_id=0, has_side_effects=True, vmem_limit_bytes=48 * 1024 * 1024
        ),
        cost_estimate=pl.CostEstimate(
            flops=4 * vectors * lc * sb * columns * sb * channels,
            bytes_accessed=4 * two_site.size + 2 * left_env.size + 2 * right_env.size,
            transcendentals=0,
        ),
    )(left_size, right_size, channel_shift, two_site, left_rows, right_rows)


def solution(mesh):
    placed = (
        P(None, "lsec", None, "rsec"),
        P(None, "lsec", "rsec", None),
        P(None, "rsec", "lsec", None),
        P("lsec"),
        P("rsec"),
        P(),
    )
    body = functools.partial(local, mesh.shape["lsec"], mesh.shape["rsec"])
    return jax.shard_map(
        body, mesh=mesh, in_specs=placed, out_specs=P(None, "lsec", None, "rsec"), check_vma=False
    )
```

```python
import functools

import jax
import jax.numpy as jnp
from jax import lax
from jax.experimental import pallas as pl
from jax.experimental.pallas import tpu as pltpu
from jax.sharding import PartitionSpec as P

SHIFT = 2
GROUP = 2
EARLY, RELAY, SECOND, THIRD = 4, 10, 8, 4
MESH = pl.DeviceIdType.MESH


def kernel(
    nl, nr, lsize, rsize, shift, x_hbm, l_hbm, r_hbm, out,
    xbuf, lbuf, rbuf, pbuf, acc,
    x_sem, own_sem, rh_send, rh_recv, lh_send, lh_recv,
    l1_send, l1_recv, l2_send, l2_recv, far_send, r1_send, r1_recv, r2_send, r2_recv,
):
    vectors, lc, sb, columns = x_hbm.shape
    rc = columns // sb
    channels = l_hbm.shape[0]
    eb = l_hbm.shape[1] // lc
    cb = r_hbm.shape[1] // rc
    chunks = channels // GROUP
    nz, ny = nr // 2, nl // 2
    lam = lax.axis_index("lsec")
    rho = lax.axis_index("rsec")
    mz, mx = rho // 2, rho % 2
    my, mc = lam // 2, lam % 2
    xpeer = mz * 2 + (1 - mx)
    cpeer = my * 2 + (1 - mc)
    S = SHIFT
    own_r, own_l = pl.ds(S, rc), pl.ds(S, lc)

    def zslot(j):
        return ((mz + (nz - j)) % nz) * 2 + mx

    def yslot(j):
        return ((my + (ny - j)) % ny) * 2 + mc

    def zto(j):
        return ((mz + j) % nz) * 2 + mx

    def yto(j):
        return ((my + j) % ny) * 2 + mc

    def remote(src, dst, send, recv, to):
        return pltpu.make_async_remote_copy(
            src_ref=src, dst_ref=dst, send_sem=send, recv_sem=recv,
            device_id=to, device_id_type=MESH,
        )

    x_copies = [
        pltpu.make_async_copy(
            x_hbm.at[:, :, :, pl.ds(r * sb, sb)], xbuf.at[S + r, :, own_l], x_sem.at[r]
        )
        for r in range(rc)
    ]
    for copy in x_copies:
        copy.start()
    own_l_copy = pltpu.make_async_copy(l_hbm, lbuf.at[rho], own_sem.at[0])
    own_r_copy = pltpu.make_async_copy(r_hbm, rbuf.at[lam], own_sem.at[1])
    own_l_copy.start()
    own_r_copy.start()

    has_up_r, has_dn_r = rho < nr - 1, rho > 0
    has_up_l, has_dn_l = lam < nl - 1, lam > 0
    far_r = jnp.where(mx == 1, rho + 1, rho + nr - 1) % nr
    far_l = jnp.where(mc == 1, lam + 1, lam + nl - 1) % nl

    barrier = pltpu.get_barrier_semaphore()
    near = [(lam, zto(j)) for j in range(1, nz)] + [(lam, xpeer)]
    near += [(yto(j), rho) for j in range(1, ny)] + [(cpeer, rho)]
    near += [(lam, far_r), (far_l, rho)]
    for to in near:
        pl.semaphore_signal(barrier, inc=1, device_id=to, device_id_type=MESH)

    def zero_r(at):
        xbuf[pl.ds(at, S)] = jnp.zeros((S,) + xbuf.shape[1:], xbuf.dtype)

    def zero_l(at):
        shape = (rc + 2 * S, vectors, S, sb, sb)
        xbuf[:, :, pl.ds(at, S)] = jnp.zeros(shape, xbuf.dtype)

    pl.when(rho == 0)(lambda: zero_r(0))
    pl.when(rho == nr - 1)(lambda: zero_r(S + rc))
    pl.when(lam == 0)(lambda: zero_l(0))
    pl.when(lam == nl - 1)(lambda: zero_l(S + lc))

    pl.semaphore_wait(barrier, len(near))

    relayed = nz == 4
    relays = (mz == 1) | (mz == 2)
    relay_to = jnp.where(mz == 2, 3, 0) * 2 + mx
    relay_sem = jnp.where(mz == 2, 3, 1)

    def near_z(j):
        if not relayed or j == 2:
            return True
        return (mz != nz - 1) if j == 1 else (mz != 0)

    def when(condition, action):
        if condition is True:
            action()
        else:
            pl.when(condition)(action)

    def by_z(c):
        return c % 3 == 2

    def part_of(c):
        return pl.ds(c * GROUP, GROUP)

    def l_first(c, j, slot=None):
        part = part_of(c)
        return remote(
            l_hbm.at[part], lbuf.at[rho if slot is None else slot, part],
            l1_send.at[c, j - 1], l1_recv.at[c, j - 1], (lam, zto(j)),
        )

    def l_own(c):
        part = part_of(c)
        return remote(
            l_hbm.at[part], lbuf.at[rho, part],
            l2_send.at[c, 0], l2_recv.at[c, 0], (lam, xpeer),
        )

    def l_relay(c):
        at = lbuf.at[zslot(2), part_of(c)]
        return remote(at, at, far_send.at[c, 0], l1_recv.at[c, relay_sem - 1], (lam, relay_to))

    def l_second_x(c, j):
        at = lbuf.at[zslot(j), part_of(c)]
        return remote(at, at, l2_send.at[c, j], l2_recv.at[c, j], (lam, xpeer))

    def l_second_z(c, j):
        at = lbuf.at[xpeer, part_of(c)]
        return remote(at, at, l2_send.at[c, j], l2_recv.at[c, j], (lam, zto(j)))

    def l_third(c):
        at = lbuf.at[((mz + (nz - 2)) % nz) * 2 + (1 - mx), part_of(c)]
        return remote(at, at, far_send.at[c, 1], l2_recv.at[c, relay_sem], (lam, relay_to))

    def l_in(c, j):
        at = lbuf.at[((mz + (nz - j)) % nz) * 2 + (1 - mx), part_of(c)]
        return remote(at, at, l2_send.at[c, j], l2_recv.at[c, j], (lam, xpeer))

    def r_first(c, j, slot=None):
        part = part_of(c)
        return remote(
            r_hbm.at[part], rbuf.at[lam if slot is None else slot, part],
            r1_send.at[c, j - 1], r1_recv.at[c, j - 1], (yto(j), rho),
        )

    def r_own(c):
        part = part_of(c)
        return remote(
            r_hbm.at[part], rbuf.at[lam, part],
            r2_send.at[c, 0], r2_recv.at[c, 0], (cpeer, rho),
        )

    def r_second(c, j):
        at = rbuf.at[yslot(j), part_of(c)]
        return remote(at, at, r2_send.at[c, j], r2_recv.at[c, j], (cpeer, rho))

    def r_in(c, j):
        at = rbuf.at[((my + (ny - j)) % ny) * 2 + (1 - mc), part_of(c)]
        return remote(at, at, r2_send.at[c, j], r2_recv.at[c, j], (cpeer, rho))

    def start_first(c):
        for j in range(1, nz):
            when(near_z(j), l_first(c, j).start)
        l_own(c).start()
        for j in range(1, ny):
            r_first(c, j).start()
        r_own(c).start()

    def relay(c):
        if relayed:
            l_first(c, 2, zslot(2)).wait_recv()
            pl.when(relays)(l_relay(c).start)

    def second(c):
        for j in range(1, ny):
            r_first(c, j, yslot(j)).wait_recv()
            r_second(c, j).start()
        l_in(c, 0).wait_recv()

        @pl.when(by_z(c))
        def _():
            for j in range(1, nz):
                when(near_z(j), l_second_z(c, j).start)

        for j in range(1, nz):
            if not (relayed and j == 2):
                l_first(c, j, zslot(j)).wait_recv()

        @pl.when(jnp.logical_not(by_z(c)))
        def _():
            for j in range(1, nz):
                l_second_x(c, j).start()

    def third(c):
        if relayed:
            @pl.when(by_z(c))
            def _():
                l_in(c, 2).wait_recv()
                pl.when(relays)(l_third(c).start)

    def arrive(c):
        for j in range(1, nz):
            if relayed and j == 2:
                pl.when(jnp.logical_not(by_z(c)))(l_in(c, j).wait_recv)
            else:
                l_in(c, j).wait_recv()
        for j in range(ny):
            r_in(c, j).wait_recv()

    def sent(c):
        for j in range(1, nz):
            when(near_z(j), l_first(c, j).wait_send)
        l_own(c).wait_send()
        for j in range(1, ny):
            r_first(c, j).wait_send()
            r_second(c, j).wait_send()
        r_own(c).wait_send()
        if relayed:
            pl.when(relays)(l_relay(c).wait_send)
            pl.when(relays & by_z(c))(l_third(c).wait_send)

        @pl.when(by_z(c))
        def _():
            for j in range(1, nz):
                when(near_z(j), l_second_z(c, j).wait_send)

        @pl.when(jnp.logical_not(by_z(c)))
        def _():
            for j in range(1, nz):
                l_second_x(c, j).wait_send()

    def each(begin, end, action):
        def body(c, carry):
            action(c)
            return carry

        lax.fori_loop(begin, end, body, 0)

    each(0, EARLY, start_first)

    rows = lax.broadcasted_iota(jnp.int32, (sb, sb), 0)
    cols = lax.broadcasted_iota(jnp.int32, (sb, sb), 1)
    for r in range(rc):
        x_copies[r].wait()
        for l in range(lc):
            live = ((rows < lsize[l]) & (cols < rsize[r])).astype(jnp.float32)
            for v in range(vectors):
                block = xbuf[S + r, v, S + l].astype(jnp.float32)
                xbuf[S + r, v, S + l] = (block * live).astype(xbuf.dtype)

    r_up = remote(
        xbuf.at[pl.ds(rc, S), :, own_l], xbuf.at[pl.ds(0, S), :, own_l],
        rh_send.at[0], rh_recv.at[0], (lam, rho + 1),
    )
    r_dn = remote(
        xbuf.at[pl.ds(S, S), :, own_l], xbuf.at[pl.ds(S + rc, S), :, own_l],
        rh_send.at[1], rh_recv.at[1], (lam, rho - 1),
    )

    def l_rim(part, at, count):
        up = remote(
            xbuf.at[pl.ds(at, count), :, pl.ds(lc, S)], xbuf.at[pl.ds(at, count), :, pl.ds(0, S)],
            lh_send.at[part, 0], lh_recv.at[part, 0], (lam + 1, rho),
        )
        dn = remote(
            xbuf.at[pl.ds(at, count), :, pl.ds(S, S)], xbuf.at[pl.ds(at, count), :, pl.ds(S + lc, S)],
            lh_send.at[part, 1], lh_recv.at[part, 1], (lam - 1, rho),
        )
        return up, dn

    l_mid = l_rim(0, S, rc)
    l_low = l_rim(1, 0, S)
    l_high = l_rim(2, S + rc, S)
    pl.when(has_up_r)(r_up.start)
    pl.when(has_dn_r)(r_dn.start)
    pl.when(has_up_l)(l_mid[0].start)
    pl.when(has_dn_l)(l_mid[1].start)

    each(EARLY, chunks, start_first)
    each(0, EARLY, relay)

    @pl.when(has_dn_r)
    def _():
        r_up.wait_recv()
        pl.when(has_up_l)(l_low[0].start)
        pl.when(has_dn_l)(l_low[1].start)

    @pl.when(has_up_r)
    def _():
        r_dn.wait_recv()
        pl.when(has_up_l)(l_high[0].start)
        pl.when(has_dn_l)(l_high[1].start)

    acc[...] = jnp.zeros_like(acc)
    own_l_copy.wait()
    own_r_copy.wait()

    each(EARLY, RELAY, relay)
    each(0, SECOND, second)
    each(0, THIRD, third)

    @pl.when(has_dn_l)
    def _():
        l_mid[0].wait_recv()
        pl.when(has_dn_r)(l_low[0].wait_recv)
        pl.when(has_up_r)(l_high[0].wait_recv)

    @pl.when(has_up_l)
    def _():
        l_mid[1].wait_recv()
        pl.when(has_dn_r)(l_low[1].wait_recv)
        pl.when(has_up_r)(l_high[1].wait_recv)

    def right_block(k, r):
        return rbuf[:, k, pl.ds(r * cb, cb), :].reshape(sb, sb)

    def left_block(k, l):
        if eb % 16 == 0:
            return lbuf[:, k, pl.ds(l * eb, eb), :].reshape(sb, sb)
        pieces = lbuf[:, k].astype(jnp.float32).reshape(nr, lc, eb, sb)
        return pieces[:, l].reshape(sb, sb).astype(jnp.bfloat16)

    def step(c, carry):
        pl.when(c + RELAY < chunks)(lambda: relay(c + RELAY))
        pl.when(c + SECOND < chunks)(lambda: second(c + SECOND))
        pl.when(c + THIRD < chunks)(lambda: third(c + THIRD))
        arrive(c)
        for g in range(GROUP):
            k = c * GROUP + g
            l_from = S - shift[k, 0]
            r_from = S - shift[k, 1]
            for r in range(rc):
                weights = right_block(k, r)
                for v in range(vectors):
                    source = xbuf[r_from + r, v, pl.ds(l_from, lc)].reshape(lc * sb, sb)
                    part = lax.dot_general(
                        source, weights, (((1,), (1,)), ((), ())),
                        preferred_element_type=jnp.float32,
                    ).astype(jnp.bfloat16)
                    pbuf[:, pl.ds(g * sb, sb), pl.ds((v * rc + r) * sb, sb)] = part.reshape(lc, sb, sb)
        for l in range(lc):
            left = jnp.concatenate(
                [left_block(c * GROUP + g, l) for g in range(GROUP)], axis=1
            )
            acc[l] += jnp.dot(left, pbuf[l], preferred_element_type=jnp.float32)
        return carry

    lax.fori_loop(0, chunks, step, 0)

    for l in range(lc):
        for r in range(rc):
            live = ((rows < lsize[l]) & (cols < rsize[r])).astype(jnp.float32)
            for v in range(vectors):
                block = acc[l, :, pl.ds((v * rc + r) * sb, sb)]
                out[v, l, :, pl.ds(r * sb, sb)] = (block * live).astype(out.dtype)

    each(0, chunks, sent)
    pl.when(has_up_r)(r_up.wait_send)
    pl.when(has_dn_r)(r_dn.wait_send)
    for pair, there in ((l_mid, None), (l_low, has_dn_r), (l_high, has_up_r)):
        for copy, to in zip(pair, (has_up_l, has_dn_l)):
            pl.when(to if there is None else to & there)(copy.wait_send)


def local(nl, nr, two_site, left_env, right_env, left_size, right_size, channel_shift):
    vectors, lc, sb, columns = two_site.shape
    channels, rc = right_env.shape[:2]
    chunks = channels // GROUP
    nz, ny = nr // 2, nl // 2
    left_rows = left_env.reshape(channels, -1, sb)
    right_rows = right_env.reshape(channels, -1, sb)
    smem = pl.BlockSpec(memory_space=pltpu.SMEM)
    hbm = pl.BlockSpec(memory_space=pl.ANY)
    dma = pltpu.SemaphoreType.DMA
    return pl.pallas_call(
        functools.partial(kernel, nl, nr),
        out_shape=jax.ShapeDtypeStruct(two_site.shape, jnp.bfloat16),
        in_specs=[smem, smem, smem, hbm, hbm, hbm],
        out_specs=pl.BlockSpec(memory_space=pltpu.VMEM),
        scratch_shapes=[
            pltpu.VMEM((rc + 2 * SHIFT, vectors, lc + 2 * SHIFT, sb, sb), jnp.bfloat16),
            pltpu.VMEM((nr,) + left_rows.shape, jnp.bfloat16),
            pltpu.VMEM((nl,) + right_rows.shape, jnp.bfloat16),
            pltpu.VMEM((lc, GROUP * sb, vectors * columns), jnp.bfloat16),
            pltpu.VMEM((lc, sb, vectors * columns), jnp.float32),
            dma((rc,)), dma((2,)), dma((2,)), dma((2,)), dma((3, 2)), dma((3, 2)),
            dma((chunks, nz - 1)), dma((chunks, nz - 1)), dma((chunks, nz)), dma((chunks, nz)),
            dma((chunks, 2)),
            dma((chunks, ny - 1)), dma((chunks, ny - 1)), dma((chunks, ny)), dma((chunks, ny)),
        ],
        compiler_params=pltpu.CompilerParams(
            collective_id=0, has_side_effects=True, vmem_limit_bytes=60 * 1024 * 1024
        ),
        cost_estimate=pl.CostEstimate(
            flops=4 * vectors * lc * sb * columns * sb * channels,
            bytes_accessed=4 * two_site.size + 2 * left_env.size + 2 * right_env.size,
            transcendentals=0,
        ),
    )(left_size, right_size, channel_shift, two_site, left_rows, right_rows)


def solution(mesh):
    placed = (
        P(None, "lsec", None, "rsec"),
        P(None, "lsec", "rsec", None),
        P(None, "rsec", "lsec", None),
        P("lsec"),
        P("rsec"),
        P(),
    )
    body = functools.partial(local, mesh.shape["lsec"], mesh.shape["rsec"])
    return jax.shard_map(
        body, mesh=mesh, in_specs=placed, out_specs=P(None, "lsec", None, "rsec"), check_vma=False
    )
```

```python
import functools

import jax
import jax.numpy as jnp
from jax import lax
from jax.experimental import pallas as pl
from jax.experimental.pallas import tpu as pltpu
from jax.sharding import PartitionSpec as P

SHIFT = 2
GROUP = 2
AHEAD = 8
MESH = pl.DeviceIdType.MESH


def kernel(
    nl, nr, lsize, rsize, shift, x_hbm, l_hbm, r_hbm, out,
    xbuf, lbuf, rbuf, pbuf, acc,
    x_sem, own_sem, rh_send, rh_recv, lh_send, lh_recv,
    l1_send, l1_recv, l2_send, l2_recv, r1_send, r1_recv, r2_send, r2_recv,
):
    vectors, lc, sb, columns = x_hbm.shape
    rc = columns // sb
    channels = l_hbm.shape[0]
    eb = l_hbm.shape[1] // lc
    cb = r_hbm.shape[1] // rc
    chunks = channels // GROUP
    nz, ny = nr // 2, nl // 2
    lam = lax.axis_index("lsec")
    rho = lax.axis_index("rsec")
    mz, mx = rho // 2, rho % 2
    my, mc = lam // 2, lam % 2
    xpeer = mz * 2 + (1 - mx)
    cpeer = my * 2 + (1 - mc)
    S = SHIFT
    own_r, own_l = pl.ds(S, rc), pl.ds(S, lc)

    def zslot(j):
        return ((mz + (nz - j)) % nz) * 2 + mx

    def yslot(j):
        return ((my + (ny - j)) % ny) * 2 + mc

    def zto(j):
        return ((mz + j) % nz) * 2 + mx

    def yto(j):
        return ((my + j) % ny) * 2 + mc

    def remote(src, dst, send, recv, to):
        return pltpu.make_async_remote_copy(
            src_ref=src, dst_ref=dst, send_sem=send, recv_sem=recv,
            device_id=to, device_id_type=MESH,
        )

    x_copies = [
        pltpu.make_async_copy(
            x_hbm.at[:, :, :, pl.ds(r * sb, sb)], xbuf.at[S + r, :, own_l], x_sem.at[r]
        )
        for r in range(rc)
    ]
    for copy in x_copies:
        copy.start()
    own_l_copy = pltpu.make_async_copy(l_hbm, lbuf.at[rho], own_sem.at[0])
    own_r_copy = pltpu.make_async_copy(r_hbm, rbuf.at[lam], own_sem.at[1])
    own_l_copy.start()
    own_r_copy.start()

    has_up_r, has_dn_r = rho < nr - 1, rho > 0
    has_up_l, has_dn_l = lam < nl - 1, lam > 0
    far_r = jnp.where(mx == 1, rho + 1, rho + nr - 1) % nr
    far_l = jnp.where(mc == 1, lam + 1, lam + nl - 1) % nl

    barrier = pltpu.get_barrier_semaphore()
    near = [(lam, zto(j)) for j in range(1, nz)] + [(lam, xpeer)]
    near += [(yto(j), rho) for j in range(1, ny)] + [(cpeer, rho)]
    near += [(lam, far_r), (far_l, rho)]
    for to in near:
        pl.semaphore_signal(barrier, inc=1, device_id=to, device_id_type=MESH)

    def zero_r(at):
        xbuf[pl.ds(at, S)] = jnp.zeros((S,) + xbuf.shape[1:], xbuf.dtype)

    def zero_l(at):
        shape = (rc + 2 * S, vectors, S, sb, sb)
        xbuf[:, :, pl.ds(at, S)] = jnp.zeros(shape, xbuf.dtype)

    pl.when(rho == 0)(lambda: zero_r(0))
    pl.when(rho == nr - 1)(lambda: zero_r(S + rc))
    pl.when(lam == 0)(lambda: zero_l(0))
    pl.when(lam == nl - 1)(lambda: zero_l(S + lc))

    rows = lax.broadcasted_iota(jnp.int32, (sb, sb), 0)
    cols = lax.broadcasted_iota(jnp.int32, (sb, sb), 1)
    for r in range(rc):
        x_copies[r].wait()
        for l in range(lc):
            live = ((rows < lsize[l]) & (cols < rsize[r])).astype(jnp.float32)
            for v in range(vectors):
                block = xbuf[S + r, v, S + l].astype(jnp.float32)
                xbuf[S + r, v, S + l] = (block * live).astype(xbuf.dtype)

    pl.semaphore_wait(barrier, len(near))

    r_up = remote(
        xbuf.at[pl.ds(rc, S), :, own_l], xbuf.at[pl.ds(0, S), :, own_l],
        rh_send.at[0], rh_recv.at[0], (lam, rho + 1),
    )
    r_dn = remote(
        xbuf.at[pl.ds(S, S), :, own_l], xbuf.at[pl.ds(S + rc, S), :, own_l],
        rh_send.at[1], rh_recv.at[1], (lam, rho - 1),
    )

    def l_rim(part, at, count):
        up = remote(
            xbuf.at[pl.ds(at, count), :, pl.ds(lc, S)], xbuf.at[pl.ds(at, count), :, pl.ds(0, S)],
            lh_send.at[part, 0], lh_recv.at[part, 0], (lam + 1, rho),
        )
        dn = remote(
            xbuf.at[pl.ds(at, count), :, pl.ds(S, S)], xbuf.at[pl.ds(at, count), :, pl.ds(S + lc, S)],
            lh_send.at[part, 1], lh_recv.at[part, 1], (lam - 1, rho),
        )
        return up, dn

    l_mid = l_rim(0, S, rc)
    l_low = l_rim(1, 0, S)
    l_high = l_rim(2, S + rc, S)
    pl.when(has_up_r)(r_up.start)
    pl.when(has_dn_r)(r_dn.start)
    pl.when(has_up_l)(l_mid[0].start)
    pl.when(has_dn_l)(l_mid[1].start)

    def first_hop(c):
        part = pl.ds(c * GROUP, GROUP)
        copies = []
        for j in range(1, nz):
            copies.append(remote(
                l_hbm.at[part], lbuf.at[rho, part],
                l1_send.at[c, j - 1], l1_recv.at[c, j - 1], (lam, zto(j)),
            ))
        for j in range(1, ny):
            copies.append(remote(
                r_hbm.at[part], rbuf.at[lam, part],
                r1_send.at[c, j - 1], r1_recv.at[c, j - 1], (yto(j), rho),
            ))
        copies.append(remote(
            l_hbm.at[part], lbuf.at[rho, part],
            l2_send.at[c, 0], l2_recv.at[c, 0], (lam, xpeer),
        ))
        copies.append(remote(
            r_hbm.at[part], rbuf.at[lam, part],
            r2_send.at[c, 0], r2_recv.at[c, 0], (cpeer, rho),
        ))
        return copies

    def first_in(c):
        part = pl.ds(c * GROUP, GROUP)
        copies = []
        for j in range(1, nz):
            copies.append(remote(
                l_hbm.at[part], lbuf.at[zslot(j), part],
                l1_send.at[c, j - 1], l1_recv.at[c, j - 1], (lam, zto(j)),
            ))
        for j in range(1, ny):
            copies.append(remote(
                r_hbm.at[part], rbuf.at[yslot(j), part],
                r1_send.at[c, j - 1], r1_recv.at[c, j - 1], (yto(j), rho),
            ))
        return copies

    def second_hop(c):
        part = pl.ds(c * GROUP, GROUP)
        copies = []
        for j in range(1, nz):
            at = lbuf.at[zslot(j), part]
            copies.append(remote(at, at, l2_send.at[c, j], l2_recv.at[c, j], (lam, xpeer)))
        for j in range(1, ny):
            at = rbuf.at[yslot(j), part]
            copies.append(remote(at, at, r2_send.at[c, j], r2_recv.at[c, j], (cpeer, rho)))
        return copies

    def second_in(c):
        part = pl.ds(c * GROUP, GROUP)
        copies = []
        for j in range(nz):
            at = lbuf.at[((mz + (nz - j)) % nz) * 2 + (1 - mx), part]
            copies.append(remote(at, at, l2_send.at[c, j], l2_recv.at[c, j], (lam, xpeer)))
        for j in range(ny):
            at = rbuf.at[((my + (ny - j)) % ny) * 2 + (1 - mc), part]
            copies.append(remote(at, at, r2_send.at[c, j], r2_recv.at[c, j], (cpeer, rho)))
        return copies

    def start_first(c):
        for copy in first_hop(c):
            copy.start()

    def forward(c):
        for copy in first_in(c):
            copy.wait_recv()
        for copy in second_hop(c):
            copy.start()

    def start_chunk(c, carry):
        start_first(c)
        return carry

    lax.fori_loop(0, chunks, start_chunk, 0)

    @pl.when(has_dn_r)
    def _():
        r_up.wait_recv()
        pl.when(has_up_l)(l_low[0].start)
        pl.when(has_dn_l)(l_low[1].start)

    @pl.when(has_up_r)
    def _():
        r_dn.wait_recv()
        pl.when(has_up_l)(l_high[0].start)
        pl.when(has_dn_l)(l_high[1].start)

    acc[...] = jnp.zeros_like(acc)
    own_l_copy.wait()
    own_r_copy.wait()

    def forward_chunk(c, carry):
        forward(c)
        return carry

    lax.fori_loop(0, AHEAD, forward_chunk, 0)

    @pl.when(has_dn_l)
    def _():
        l_mid[0].wait_recv()
        pl.when(has_dn_r)(l_low[0].wait_recv)
        pl.when(has_up_r)(l_high[0].wait_recv)

    @pl.when(has_up_l)
    def _():
        l_mid[1].wait_recv()
        pl.when(has_dn_r)(l_low[1].wait_recv)
        pl.when(has_up_r)(l_high[1].wait_recv)

    def right_block(k, r):
        return rbuf[:, k, pl.ds(r * cb, cb), :].reshape(sb, sb)

    def left_block(k, l):
        if eb % 16 == 0:
            return lbuf[:, k, pl.ds(l * eb, eb), :].reshape(sb, sb)
        pieces = lbuf[:, k].astype(jnp.float32).reshape(nr, lc, eb, sb)
        return pieces[:, l].reshape(sb, sb).astype(jnp.bfloat16)

    def step(c, carry):
        @pl.when(c + AHEAD < chunks)
        def _():
            forward(c + AHEAD)

        for copy in second_in(c):
            copy.wait_recv()
        for g in range(GROUP):
            k = c * GROUP + g
            l_from = S - shift[k, 0]
            r_from = S - shift[k, 1]
            for r in range(rc):
                weights = right_block(k, r)
                for v in range(vectors):
                    source = xbuf[r_from + r, v, pl.ds(l_from, lc)].reshape(lc * sb, sb)
                    part = lax.dot_general(
                        source, weights, (((1,), (1,)), ((), ())),
                        preferred_element_type=jnp.float32,
                    ).astype(jnp.bfloat16)
                    pbuf[:, pl.ds(g * sb, sb), pl.ds((v * rc + r) * sb, sb)] = part.reshape(lc, sb, sb)
        for l in range(lc):
            left = jnp.concatenate(
                [left_block(c * GROUP + g, l) for g in range(GROUP)], axis=1
            )
            acc[l] += jnp.dot(left, pbuf[l], preferred_element_type=jnp.float32)
        return carry

    lax.fori_loop(0, chunks, step, 0)

    for l in range(lc):
        for r in range(rc):
            live = ((rows < lsize[l]) & (cols < rsize[r])).astype(jnp.float32)
            for v in range(vectors):
                block = acc[l, :, pl.ds((v * rc + r) * sb, sb)]
                out[v, l, :, pl.ds(r * sb, sb)] = (block * live).astype(out.dtype)

    def drain(c, carry):
        for copy in first_hop(c) + second_hop(c):
            copy.wait_send()
        return carry

    lax.fori_loop(0, chunks, drain, 0)
    pl.when(has_up_r)(r_up.wait_send)
    pl.when(has_dn_r)(r_dn.wait_send)
    for pair, there in ((l_mid, None), (l_low, has_dn_r), (l_high, has_up_r)):
        for copy, to in zip(pair, (has_up_l, has_dn_l)):
            pl.when(to if there is None else to & there)(copy.wait_send)


def local(nl, nr, two_site, left_env, right_env, left_size, right_size, channel_shift):
    vectors, lc, sb, columns = two_site.shape
    channels, rc = right_env.shape[:2]
    chunks = channels // GROUP
    nz, ny = nr // 2, nl // 2
    left_rows = left_env.reshape(channels, -1, sb)
    right_rows = right_env.reshape(channels, -1, sb)
    smem = pl.BlockSpec(memory_space=pltpu.SMEM)
    hbm = pl.BlockSpec(memory_space=pl.ANY)
    dma = pltpu.SemaphoreType.DMA
    return pl.pallas_call(
        functools.partial(kernel, nl, nr),
        out_shape=jax.ShapeDtypeStruct(two_site.shape, jnp.bfloat16),
        in_specs=[smem, smem, smem, hbm, hbm, hbm],
        out_specs=pl.BlockSpec(memory_space=pltpu.VMEM),
        scratch_shapes=[
            pltpu.VMEM((rc + 2 * SHIFT, vectors, lc + 2 * SHIFT, sb, sb), jnp.bfloat16),
            pltpu.VMEM((nr,) + left_rows.shape, jnp.bfloat16),
            pltpu.VMEM((nl,) + right_rows.shape, jnp.bfloat16),
            pltpu.VMEM((lc, GROUP * sb, vectors * columns), jnp.bfloat16),
            pltpu.VMEM((lc, sb, vectors * columns), jnp.float32),
            dma((rc,)), dma((2,)), dma((2,)), dma((2,)), dma((3, 2)), dma((3, 2)),
            dma((chunks, nz - 1)), dma((chunks, nz - 1)), dma((chunks, nz)), dma((chunks, nz)),
            dma((chunks, ny - 1)), dma((chunks, ny - 1)), dma((chunks, ny)), dma((chunks, ny)),
        ],
        compiler_params=pltpu.CompilerParams(
            collective_id=0, has_side_effects=True, vmem_limit_bytes=60 * 1024 * 1024
        ),
        cost_estimate=pl.CostEstimate(
            flops=4 * vectors * lc * sb * columns * sb * channels,
            bytes_accessed=4 * two_site.size + 2 * left_env.size + 2 * right_env.size,
            transcendentals=0,
        ),
    )(left_size, right_size, channel_shift, two_site, left_rows, right_rows)


def solution(mesh):
    placed = (
        P(None, "lsec", None, "rsec"),
        P(None, "lsec", "rsec", None),
        P(None, "rsec", "lsec", None),
        P("lsec"),
        P("rsec"),
        P(),
    )
    body = functools.partial(local, mesh.shape["lsec"], mesh.shape["rsec"])
    return jax.shard_map(
        body, mesh=mesh, in_specs=placed, out_specs=P(None, "lsec", None, "rsec"), check_vma=False
    )
```
